256 devices in a mesh: tok: 32 (over x, y, z_hi), blk: 8 (over z_lo, core).
Axes of the slice: x: 4, y: 4, z: 8 (z_hi: 2, z_lo: 4; z = z_hi * 4 + z_lo), core: 2. Of those that a mesh axis runs over, the one named last changes fastest.
Arguments:
- activations: bfloat16 [2048, 4096], P('tok', 'blk'), may hold values from -40 to 40
- gradients: bfloat16 [2048, 14336], P('tok', 'blk'), may hold values from -40 to 40
- input_basis: bfloat16 [4096, 4096], P('tok', 'blk'), may hold values from -0.09375 to 0.09375
- output_basis: bfloat16 [14336, 14336], P('blk', 'tok'), may hold values from -0.046875 to 0.046875
Outputs:
- input_covariance: float32 [4096, 4096], P('blk', 'tok')
- output_covariance: float32 [14336, 14336], P('blk', 'tok')
- corrections: float32 [4096, 14336], P('blk', 'tok')
The draws below stay inside these ranges and needn't reach their ends.
All inputs are finite; a program needn't handle non-finite values.
Results may differ from the reference program's by a relative error of at most 0.00046.
Values may be sent and summed in bfloat16 or wider, within the bound.
No kernel may reach another device: no remote copies, remote signals or barrier semaphores. Data moves between devices by JAX's collectives and lax.ppermute only.
A program may use at most 128 MiB of HBM per device.

```python
import jax
import jax.numpy as jnp

D = 4096
FF = 14336
TOKENS = 2048


def scaled_field(seed_key, row_count, col_count, spread, noise):
    row_key, col_key = jax.random.split(seed_key, 2)
    row_scale = jnp.exp(jax.random.uniform(row_key, (row_count, 1), jnp.float32, -spread, spread))
    col_scale = jnp.exp(jax.random.uniform(col_key, (1, col_count), jnp.float32, -spread, spread))
    return jnp.clip(noise * row_scale * col_scale, -40.0, 40.0)


def draw_activations(key, part):
    key = jax.random.fold_in(key, 5)
    noise_key, scale_key = jax.random.split(key)
    noise = jax.random.normal(noise_key, (TOKENS, D), jnp.float32)
    return scaled_field(scale_key, TOKENS, D, 0.8, noise).astype(jnp.bfloat16)


def draw_gradients(key, part):
    key = jax.random.fold_in(key, 9)
    noise_key, scale_key = jax.random.split(key)
    noise = jax.random.normal(noise_key, (TOKENS, FF), jnp.float32)
    return scaled_field(scale_key, TOKENS, FF, 0.8, noise).astype(jnp.bfloat16)


def level_of(own_key, shape, shards, smallest, largest):
    gain, own = 1.0, jax.random.fold_in(own_key, 6)
    for axis_at, blocks in shards:
        steps = jnp.exp(jax.random.uniform(jax.random.fold_in(own, axis_at), (blocks,), jnp.float32, smallest / len(shards), largest / len(shards)))
        gain = gain * jnp.repeat(steps, shape[axis_at] // blocks).reshape([-1 if axis == axis_at else 1 for axis in range(len(shape))])
    return gain


def normal_values(rng, extent, scale, limit, pieces=(), held_as=jnp.bfloat16):
    array = jax.random.normal(rng, extent, jnp.float32) * scale
    if len(pieces) > 0:
        array = level_of(rng, extent, pieces, -0.22, 0.18) * array
    return jnp.clip(array, min=-limit, max=limit).astype(held_as)


def setup_inputs(seed: int = 0) -> dict:
    arg_keys = jax.random.split(jax.random.key(seed), 5)
    activations = draw_activations(jax.random.fold_in(arg_keys[4], 71), 0)
    gradients = draw_gradients(jax.random.fold_in(arg_keys[4], 71), 0)
    input_basis = normal_values(arg_keys[2], (D, D), D ** -0.5, 0.09375, ((0, 32), (1, 8)))
    output_basis = normal_values(arg_keys[3], (FF, FF), FF ** -0.5, 0.046875, ((0, 8), (1, 32)))
    return {"activations": activations, "gradients": gradients, "input_basis": input_basis, "output_basis": output_basis}


def reference(activations, gradients, input_basis, output_basis):
    input_covariance = jnp.dot(activations.T, activations, preferred_element_type=jnp.float32) / TOKENS
    output_covariance = jnp.dot(gradients.T, gradients, preferred_element_type=jnp.float32) / TOKENS
    projected_in = jnp.dot(activations, input_basis, preferred_element_type=jnp.float32)
    projected_out = jnp.dot(gradients, output_basis, preferred_element_type=jnp.float32)
    in_squares = (projected_in * projected_in).astype(jnp.bfloat16)
    out_squares = (projected_out * projected_out).astype(jnp.bfloat16)
    corrections = jnp.dot(in_squares.T, out_squares, preferred_element_type=jnp.float32) / TOKENS
    return (input_covariance, output_covariance, corrections)
```

```python
import functools

import jax
import jax.numpy as jnp
from jax import lax
from jax.experimental import pallas as pl
from jax.experimental.pallas import tpu as pltpu
from jax.sharding import Mesh
from jax.sharding import PartitionSpec as P

AXES = ("x", "y", "h", "l", "c")
SIZES = (4, 4, 2, 4, 2)
RING = 4


def after(value, *others):
    return lax.optimization_barrier((value, others))[0]


def swap(block, axis, bit):
    size = SIZES[AXES.index(axis)]
    return lax.ppermute(block, axis, [(i, i ^ bit) for i in range(size)])


def turn(block, axis, step):
    return lax.ppermute(block, axis, [(i, (i + step) % RING) for i in range(RING)])


def line(block, step):
    return lax.ppermute(block, "l", [(i, i + step) for i in range(RING) if 0 <= i + step < RING])


def copies(moves, out_shapes, *operands):
    count = len(moves(0, 0))

    def kernel(*refs):
        ins, outs, sems = refs[: len(operands)], refs[len(operands) : -1], refs[-1]
        started = [
            pltpu.make_async_copy(ins[i].at[at], outs[o].at[to], sems.at[n])
            for n, (i, at, o, to) in enumerate(moves(lax.axis_index("x"), lax.axis_index("y")))
        ]
        for copy in started:
            copy.start()
        for copy in started:
            copy.wait()

    dtype = operands[0].dtype
    total = sum(functools.reduce(lambda a, b: a * b, shape) for shape in out_shapes) * 2
    return pl.pallas_call(
        kernel,
        out_shape=[jax.ShapeDtypeStruct(shape, dtype) for shape in out_shapes],
        in_specs=[pl.BlockSpec(memory_space=pl.ANY)] * len(operands),
        out_specs=[pl.BlockSpec(memory_space=pltpu.VMEM)] * len(out_shapes),
        scratch_shapes=[pltpu.SemaphoreType.DMA((count,))],
        compiler_params=pltpu.CompilerParams(vmem_limit_bytes=2 * total + (4 << 20)),
        cost_estimate=pl.CostEstimate(flops=0, bytes_accessed=2 * total, transcendentals=0),
    )(*operands)


def near(block, axis):
    return turn(block, axis, -1), turn(block, axis, 1)


def halves(following, previous):
    rows, cols = following.shape
    half = rows // 2

    def moves(x, y):
        return [
            (0, pl.ds(0, half), 0, pl.ds(0, half)),
            (1, pl.ds(half, half), 1, pl.ds(0, half)),
        ]

    return copies(moves, [(half, cols)] * 2, previous, following)


def opposite(upper, lower, axis):
    return turn(upper, axis, 1), turn(lower, axis, -1)


def first_ring(blocks, along_y):
    size, cols = blocks[0].shape

    def moves(x, y):
        place = y if along_y else x
        at = [lax.rem(place + step, RING) * size for step in range(RING)]
        spans = ((at[0], size), (at[1], size), (at[2], size // 2), (at[2] + size // 2, size // 2), (at[3], size))
        return [(i, pl.ds(0, length), 0, pl.ds(start, length)) for i, (start, length) in enumerate(spans)]

    return copies(moves, [(4 * size, cols)], *blocks)[0]


def second_rings(a_blocks, b_blocks):
    size, cols = a_blocks[0].shape[0] // 4, a_blocks[0].shape[1]

    def moves(x, y):
        first, found = lax.axis_index("c"), []
        for n, place in enumerate((y, x)):
            base = lax.rem(first + n, 2) * 16
            for i, (step, parts) in enumerate(((0, range(4)), (1, range(4)), (2, (0, 1)), (2, (2, 3)), (3, range(4)))):
                outer = lax.rem(place + step, RING)
                for k, inner in enumerate(parts):
                    at = base + (inner * 4 + outer if n == 0 else outer * 4 + inner)
                    found.append((5 * n + i, pl.ds(k * size, size), 0, pl.ds(at * size, size)))
        return found

    return copies(moves, [(32 * size, cols)], *a_blocks, *b_blocks)[0]


def pick(rows, bit):
    half = rows.shape[0] // 2
    return (
        lax.dynamic_slice_in_dim(rows, bit * half, half),
        lax.dynamic_slice_in_dim(rows, (1 - bit) * half, half),
    )


def join(mine, other, bit):
    return jnp.where(bit == 0, jnp.concatenate([mine, other]), jnp.concatenate([other, mine]))


def swap_half(rows, exponent, axis, bit, mask):
    mine, other = pick(rows, bit)
    sent = (other * jnp.exp2(13.0 - exponent)).astype(jnp.float16)
    got = swap(sent, axis, mask), swap(jnp.full((8, 128), exponent), axis, mask)
    return mine, sent, got


def add_half(mine, got, exponent):
    rows, theirs = got
    theirs = theirs[0, 0]
    return mine + rows.astype(jnp.float32) * jnp.exp2(theirs - 13.0), jnp.maximum(exponent, theirs) + 1.0


def matmul(left, right):
    return jnp.dot(left, right, preferred_element_type=jnp.float32)


def cross_product(left, right):
    return lax.dot_general(
        left, right, (((0,), (0,)), ((), ())), preferred_element_type=jnp.float32
    )


def local(activations, gradients, input_basis, output_basis):
    x, y, h, l, c = (lax.axis_index(axis) for axis in AXES)
    rows, act_width = activations.shape
    grad_width = gradients.shape[1]
    total_rows = rows * 32
    grad_part, act_part = grad_width // 4, act_width // 4
    part = grad_part + act_part

    partner = swap(gradients, "h", 1)
    partner_acts = swap(activations, "h", 1)
    basis = lax.all_gather(input_basis, ("x", "y"), axis=0, tiled=True)
    a_next, a_prev = near(gradients, "x")
    a_up, a_down = opposite(*halves(a_next, a_prev), "x")
    b_next, b_prev = near(partner, "y")

    def wanted(grads, acts, j):
        return [
            lax.dynamic_slice_in_dim(grads, (2 * j + h) * grad_part, grad_part, 1),
            lax.dynamic_slice_in_dim(acts, (2 * j + h) * act_part, act_part, 1),
        ]

    lines = jnp.stack(
        [
            jnp.concatenate(wanted(grads, acts, j), axis=1)
            for grads, acts in ((gradients, activations), (partner, partner_acts))
            for j in range(2)
        ]
    )[None]
    lines = after(lines, a_next, a_prev)
    lines = join(lines, after(swap(lines, "l", 1), b_next, b_prev), l & 1)
    b_up, b_down = opposite(*halves(b_next, b_prev), "y")
    a_up, a_down = after((a_up, a_down), lines)
    first_a = first_ring((gradients, a_next, a_up, a_down, a_prev), False)
    first_b = first_ring((partner, b_next, b_up, b_down, b_prev), True)
    first_a, first_b = lax.optimization_barrier((first_a, first_b))
    a_next, a_prev = near(first_a, "y")
    b_next, b_prev = near(first_b, "x")
    a_halves, b_halves = halves(a_next, a_prev), halves(b_next, b_prev)
    a_up, a_down = opposite(*a_halves, "y")
    b_up, b_down = opposite(*b_halves, "x")
    other_lines = after(swap(lines, "l", 2), a_halves, b_halves)
    lines = join(lines, other_lines, l >> 1).reshape(4, 2, 2, rows, part)

    mine = lax.dynamic_index_in_dim(lines, c, 1, keepdims=False)
    other = swap(lax.dynamic_index_in_dim(lines, 1 - c, 1, keepdims=False), "c", 1)
    sides = jnp.where(c == 0, jnp.stack([mine, other], 1), jnp.stack([other, mine], 1))
    sides = sides.reshape(16, rows, part)

    act_rows = sides[:, :, grad_part:].transpose(1, 0, 2).reshape(rows, 16 * act_part)
    act_rows = jnp.concatenate([act_rows, swap(act_rows, "c", 1)])
    part_in = matmul(act_rows, basis)
    other_in = swap(part_in, "h", 1)

    grads = second_rings(
        (first_a, a_next, a_up, a_down, a_prev), (first_b, b_next, b_up, b_down, b_prev)
    )
    half = total_rows // 2
    part_out = matmul(after(grads[half:], part_in), output_basis)
    sums = matmul(after(grads[:half], part_out), output_basis)

    other_in = after(other_in, sums)
    projected_in = part_in + jnp.concatenate([other_in[rows:], other_in[:rows]])
    in_squares = (projected_in * projected_in).astype(jnp.bfloat16)
    shared = jnp.concatenate([in_squares, join(activations, partner_acts, c)], axis=1)

    sums += swap(part_out, "c", 1)
    exponent = jnp.ceil(jnp.log2(jnp.maximum(jnp.max(jnp.abs(sums)), 1e-30)))
    mine, sent, got = swap_half(sums, exponent, "l", l & 1, 1)
    shared = lax.all_gather(after(shared, sent), ("x", "y"), axis=0)
    shared = shared.reshape(16, 2, rows, 2 * act_width)
    sides = lax.all_to_all(after(sides, sent), ("x", "y"), 0, 0, tiled=True).reshape(half, part)
    sums, exponent = add_half(mine, got, exponent)
    mine, sent, got = swap_half(sums, exponent, "l", l >> 1, 2)
    sides = after(sides, sent)
    sides = jnp.concatenate([sides, swap(sides, "c", 1)])
    sums, _ = add_half(mine, after(got, sides), exponent)
    squares = (sums * sums).astype(jnp.bfloat16)
    other_squares = swap(squares, "l", 2)
    output_covariance = cross_product(grads, after(sides, squares)[:, :grad_part]) / total_rows
    squares = join(squares, after(other_squares, output_covariance), l >> 1)
    other_squares = swap(squares, "l", 1)
    shared = after(shared, squares)
    input_covariance = sum(
        cross_product(
            shared[:, i, :, act_width:].reshape(half, act_width),
            sides[i * half : (i + 1) * half, grad_part:],
        )
        for i in range(2)
    ) / total_rows
    in_squares = [shared[:, i, :, :act_width].reshape(half, act_width) for i in range(2)]
    other_squares = after(other_squares, input_covariance, *in_squares)
    squares = join(squares, other_squares, l & 1)
    other_squares = swap(squares, "c", 1)
    corrections = cross_product(in_squares[0], squares) + cross_product(in_squares[1], other_squares)
    return input_covariance, output_covariance, corrections / total_rows


def solution(mesh):
    fine = Mesh(mesh.devices.reshape(SIZES), AXES)
    tok, blk = ("x", "y", "h"), ("l", "c")
    return jax.shard_map(
        local,
        mesh=fine,
        in_specs=(P(tok, blk), P(tok, blk), P(tok, blk), P(blk, tok)),
        out_specs=(P(blk, tok), P(blk, tok), P(blk, tok)),
        check_vma=False,
    )
```

```python
import functools

import jax
import jax.numpy as jnp
from jax import lax
from jax.experimental import pallas as pl
from jax.experimental.pallas import tpu as pltpu
from jax.sharding import Mesh
from jax.sharding import PartitionSpec as P

AXES = ("x", "y", "h", "l", "c")
SIZES = (4, 4, 2, 4, 2)
RING = 4


def after(value, *others):
    return lax.optimization_barrier((value, others))[0]


def soon(array, *others):
    return after(array[:16, :128], *others) * 2


def swap(block, axis, bit):
    size = SIZES[AXES.index(axis)]
    return lax.ppermute(block, axis, [(i, i ^ bit) for i in range(size)])


def turn(block, axis, step):
    return lax.ppermute(block, axis, [(i, (i + step) % RING) for i in range(RING)])


def line(block, step):
    return lax.ppermute(block, "l", [(i, i + step) for i in range(RING) if 0 <= i + step < RING])


def copies(moves, out_shapes, *operands):
    count = len(moves(0, 0))

    def kernel(*refs):
        ins, outs, sems = refs[: len(operands)], refs[len(operands) : -1], refs[-1]
        started = [
            pltpu.make_async_copy(ins[i].at[at], outs[o].at[to], sems.at[n])
            for n, (i, at, o, to) in enumerate(moves(lax.axis_index("x"), lax.axis_index("y")))
        ]
        for copy in started:
            copy.start()
        for copy in started:
            copy.wait()

    dtype = operands[0].dtype
    total = sum(functools.reduce(lambda a, b: a * b, shape) for shape in out_shapes) * 2
    return pl.pallas_call(
        kernel,
        out_shape=[jax.ShapeDtypeStruct(shape, dtype) for shape in out_shapes],
        in_specs=[pl.BlockSpec(memory_space=pltpu.HBM)] * len(operands),
        out_specs=[pl.BlockSpec(memory_space=pltpu.VMEM)] * len(out_shapes),
        scratch_shapes=[pltpu.SemaphoreType.DMA((count,))],
        compiler_params=pltpu.CompilerParams(vmem_limit_bytes=2 * total + (4 << 20)),
        cost_estimate=pl.CostEstimate(flops=0, bytes_accessed=2 * total, transcendentals=0),
    )(*operands)


def near(block, axis):
    return turn(block, axis, -1), turn(block, axis, 1)


def halves(*pairs):
    count, (rows, cols) = 2 * len(pairs), pairs[0][0].shape
    half = rows // 2

    def kernel(*refs):
        ins, outs, held, sems = refs[:count], refs[count : 2 * count], refs[-2], refs[-1]
        loads = [
            pltpu.make_async_copy(ins[n ^ 1].at[pl.ds(n % 2 * half, half)], held.at[n], sems.at[0, n])
            for n in range(count)
        ]
        stores = [pltpu.make_async_copy(held.at[n], outs[n], sems.at[1, n]) for n in range(count)]
        for load in loads:
            load.start()
        for load, store in zip(loads, stores):
            load.wait()
            store.start()
        for store in stores:
            store.wait()

    dtype = pairs[0][0].dtype
    return pl.pallas_call(
        kernel,
        out_shape=[jax.ShapeDtypeStruct((half, cols), dtype)] * count,
        in_specs=[pl.BlockSpec(memory_space=pltpu.HBM)] * count,
        out_specs=[pl.BlockSpec(memory_space=pltpu.HBM)] * count,
        scratch_shapes=[
            pltpu.VMEM((count, half, cols), dtype),
            pltpu.SemaphoreType.DMA((2, count)),
        ],
        compiler_params=pltpu.CompilerParams(vmem_limit_bytes=12 << 20),
        cost_estimate=pl.CostEstimate(flops=0, bytes_accessed=4 * count * half * cols, transcendentals=0),
    )(*(block for pair in pairs for block in pair))


def opposite(upper, lower, axis):
    return turn(upper, axis, 1), turn(lower, axis, -1)


def first_ring(blocks, along_y):
    size, cols = blocks[0].shape

    def moves(x, y):
        place = y if along_y else x
        at = [lax.rem(place + step, RING) * size for step in range(RING)]
        spans = ((at[0], size), (at[1], size), (at[2], size // 2), (at[2] + size // 2, size // 2), (at[3], size))
        return [(i, pl.ds(0, length), 0, pl.ds(start, length)) for i, (start, length) in enumerate(spans)]

    return copies(moves, [(4 * size, cols)], *blocks)[0]


def second_moves(place, along_y, size):
    found = []
    for i, (step, parts) in enumerate(((0, range(4)), (1, range(4)), (2, (0, 1)), (2, (2, 3)), (3, range(4)))):
        outer = lax.rem(place + step, RING)
        for k, inner in enumerate(parts):
            at = inner * 4 + outer if along_y else outer * 4 + inner
            found.append((i, pl.ds(k * size, size), at * size))
    return found


def second_rings(a_blocks, b_blocks):
    size, cols = a_blocks[0].shape[0] // 4, a_blocks[0].shape[1]
    count = len(second_moves(0, True, size))

    def kernel(*refs):
        blocks, outs, sems = refs[:10], refs[10:12], refs[12]
        c = lax.axis_index("c")

        def move(n, out):
            moves = second_moves(lax.axis_index("y" if n == 0 else "x"), n == 0, size)
            return [
                pltpu.make_async_copy(blocks[5 * n + i].at[at], out.at[pl.ds(to, size)], sems.at[n, m])
                for m, (i, at, to) in enumerate(moves)
            ]

        for first in range(2):

            @pl.when(c == first)
            def _(first=first):
                started = move(first, outs[0]) + move(1 - first, outs[1])
                for copy in started:
                    copy.start()
                for copy in started:
                    copy.wait()

    return pl.pallas_call(
        kernel,
        out_shape=[jax.ShapeDtypeStruct((16 * size, cols), a_blocks[0].dtype)] * 2,
        in_specs=[pl.BlockSpec(memory_space=pltpu.HBM)] * 10,
        out_specs=[pl.BlockSpec(memory_space=pltpu.VMEM)] * 2,
        scratch_shapes=[pltpu.SemaphoreType.DMA((2, count))],
        compiler_params=pltpu.CompilerParams(vmem_limit_bytes=20 << 20),
        cost_estimate=pl.CostEstimate(flops=0, bytes_accessed=128 * size * cols, transcendentals=0),
    )(*a_blocks, *b_blocks)


def pick(rows, bit):
    half = rows.shape[0] // 2
    return (
        lax.dynamic_slice_in_dim(rows, bit * half, half),
        lax.dynamic_slice_in_dim(rows, (1 - bit) * half, half),
    )


def join(mine, other, bit):
    return jnp.where(bit == 0, jnp.concatenate([mine, other]), jnp.concatenate([other, mine]))


def swap_half(rows, exponent, axis, bit, mask):
    (mine, other), (kept, given) = pick(rows, bit), pick(exponent, bit)
    width = other.shape[1]
    wide = jnp.pad(other, ((0, 0), (0, 16)))
    inside = lax.broadcasted_iota(jnp.int32, wide.shape, 1) < width
    sent = jnp.where(inside, wide * jnp.exp2(13.0 - given), given).astype(jnp.float16)
    return mine, kept, sent, swap(sent, axis, mask)


def add_half(mine, kept, got):
    width = mine.shape[1]
    theirs = got[:, width : width + 1].astype(jnp.float32)
    sums = mine + got[:, :width].astype(jnp.float32) * jnp.exp2(theirs - 13.0)
    return sums, jnp.maximum(kept, theirs) + 1.0


def matmul(left, right):
    return jnp.dot(left, right, preferred_element_type=jnp.float32)


def cross_product(left, right):
    return lax.dot_general(
        left, right, (((0,), (0,)), ((), ())), preferred_element_type=jnp.float32
    )


def local(activations, gradients, input_basis, output_basis):
    x, y, h, l, c = (lax.axis_index(axis) for axis in AXES)
    rows, act_width = activations.shape
    grad_width = gradients.shape[1]
    total_rows = rows * 32
    grad_part, act_part = grad_width // 4, act_width // 4
    part = grad_part + act_part

    partner = swap(gradients, "h", 1)
    partner_acts = swap(activations, "h", 1)
    basis = lax.all_gather(input_basis, ("x", "y"), axis=0, tiled=True)
    a_next, a_prev = near(gradients, "x")
    a_up, a_down = opposite(*halves((a_next, a_prev)), "x")
    b_next, b_prev = near(partner, "y")

    def owned(array, width):
        cols = [lax.dynamic_slice_in_dim(array, (2 * j + h) * width, width, 1) for j in range(2)]
        return jnp.stack(cols)[None]

    acts = jnp.concatenate([activations, partner_acts])
    lines = after(owned(acts, act_part), a_next, a_prev)
    lines = join(lines, after(swap(lines, "l", 1), b_next, b_prev), l & 1)
    b_up, b_down = opposite(*halves((b_next, b_prev)), "y")
    a_up, a_down = after((a_up, a_down), lines)
    first_a = first_ring((gradients, a_next, a_up, a_down, a_prev), False)
    first_b = first_ring((partner, b_next, b_up, b_down, b_prev), True)
    first_a, first_b = lax.optimization_barrier((first_a, first_b))
    a_next, a_prev = near(first_a, "y")
    b_next, b_prev = near(first_b, "x")

    lines = after(lines, first_a, first_b)
    lines = join(lines, after(swap(lines, "l", 2), basis), l >> 1)
    other = swap(lines, "c", 1)
    act_rows = jnp.where(c == 0, jnp.stack([lines, other], 1), jnp.stack([other, lines], 1))
    act_rows = act_rows.reshape(16, 2 * rows, act_part).swapaxes(0, 1).reshape(2 * rows, 16 * act_part)
    part_in = matmul(act_rows, basis)
    other_in = swap(part_in, "h", 1)

    lines = after(jnp.concatenate([owned(gradients, grad_part), owned(partner, grad_part)]), first_a, first_b)
    lines = lines[None]
    lines = join(lines, after(swap(lines, "l", 2), part_in), l >> 1)
    other_lines = swap(lines, "l", 1)

    a_next, a_prev, b_next, b_prev = after((a_next, a_prev, b_next, b_prev), part_in, lines)
    far_halves = halves((a_next, a_prev), (b_next, b_prev))
    a_up, a_down = opposite(*far_halves[:2], "y")
    b_up, b_down = opposite(*far_halves[2:], "x")
    other_in = after(other_in, other_lines)
    projected_in = part_in + jnp.concatenate([other_in[rows:], other_in[:rows]])
    in_squares = (projected_in * projected_in).astype(jnp.bfloat16)
    shared = jnp.concatenate([in_squares, acts], axis=1)
    a_up, a_down, b_up, b_down = after((a_up, a_down, b_up, b_down), shared)
    shared = lax.all_gather(shared, ("x", "y"), axis=0).reshape(16, 2, rows, 2 * act_width)

    half = total_rows // 2
    grads, grads_rest = second_rings(
        (first_a, a_next, a_up, a_down, a_prev), (first_b, b_next, b_up, b_down, b_prev)
    )
    part_out = matmul(grads_rest, output_basis)
    kept = matmul(after(grads, part_out), output_basis)
    sums = kept + swap(part_out, "c", 1)
    exponent = jnp.max(jnp.abs(sums), axis=1, keepdims=True)
    exponent = jnp.ceil(jnp.log2(jnp.maximum(exponent, 1e-30)))
    *mine, sent, got = swap_half(sums, exponent, "l", l & 1, 1)

    started = soon(gradients, sent)
    lines, other_lines = after((lines, other_lines), started)
    lines = jnp.where(l & 1 == 0, jnp.stack([lines, other_lines], 1), jnp.stack([other_lines, lines], 1))
    lines = lines.reshape(4, 2, 2, rows, grad_part)
    mine_lines = jnp.where(c == 0, lines[:, 0], lines[:, 1])
    other = swap(jnp.where(c == 0, lines[:, 1], lines[:, 0]), "c", 1)
    sides = jnp.where(c == 0, jnp.stack([mine_lines, other], 1), jnp.stack([other, mine_lines], 1))
    sides = sides.reshape(16, rows, grad_part)
    act_sides = jnp.where(c == 0, act_rows[:rows], act_rows[rows:])
    act_sides = act_sides.reshape(rows, 16, act_part).swapaxes(0, 1)
    sides = jnp.concatenate([sides, act_sides], axis=2)
    sides = lax.all_to_all(sides, ("x", "y"), 0, 0, tiled=True).reshape(half, grad_part + act_part)

    *mine, sent, got = swap_half(*add_half(*mine, got), "l", l >> 1, 2)
    sums, _ = add_half(*mine, got)
    squares = (sums * sums).astype(jnp.bfloat16)
    line_one, line_two = swap(squares, "l", 1), swap(squares, "l", 2)
    sides, shared = after((sides, shared), soon(gradients, squares))
    sides_rest = swap(sides, "c", 1)
    shared = [lax.dynamic_index_in_dim(shared, i, 1, keepdims=False).reshape(half, -1) for i in (c, 1 - c)]
    output_covariance = cross_product(grads, sides[:, :grad_part])
    line_two = after(line_two, output_covariance, sides_rest)
    line_three = swap(line_two, "l", 1)
    shared, sides_rest = after((shared, sides_rest), line_two)
    output_covariance += cross_product(grads_rest, sides_rest[:, :grad_part])
    output_covariance /= total_rows
    input_covariance = sum(
        cross_product(block[:, act_width:], side[:, grad_part:])
        for block, side in zip(shared, (sides, sides_rest))
    ) / total_rows
    line_three = after(line_three, output_covariance, input_covariance)
    squares = join(join(squares, line_two, l >> 1), join(line_one, line_three, l >> 1), l & 1)
    squares_rest = swap(squares, "c", 1)
    corrections = sum(
        cross_product(block[:, :act_width], out) for block, out in zip(shared, (squares, squares_rest))
    )
    return input_covariance, output_covariance, corrections / total_rows


def solution(mesh):
    fine = Mesh(mesh.devices.reshape(SIZES), AXES)
    tok, blk = ("x", "y", "h"), ("l", "c")
    return jax.shard_map(
        local,
        mesh=fine,
        in_specs=(P(tok, blk), P(tok, blk), P(tok, blk), P(blk, tok)),
        out_specs=(P(blk, tok), P(blk, tok), P(blk, tok)),
        check_vma=False,
    )
```

```python
import functools

import jax
import jax.numpy as jnp
from jax import lax
from jax.experimental import pallas as pl
from jax.experimental.pallas import tpu as pltpu
from jax.sharding import Mesh
from jax.sharding import PartitionSpec as P

AXES = ("x", "y", "h", "l", "c")
SIZES = (4, 4, 2, 4, 2)
RING = 4


def after(value, *others):
    return lax.optimization_barrier((value, others))[0]


def soon(array, *others):
    return after(array[:16, :128], *others) * 2


def swap(block, axis, bit):
    size = SIZES[AXES.index(axis)]
    return lax.ppermute(block, axis, [(i, i ^ bit) for i in range(size)])


def turn(block, axis, step):
    return lax.ppermute(block, axis, [(i, (i + step) % RING) for i in range(RING)])


def line(block, step):
    return lax.ppermute(block, "l", [(i, i + step) for i in range(RING) if 0 <= i + step < RING])


def copies(moves, out_shapes, *operands):
    count = len(moves(0, 0))

    def kernel(*refs):
        ins, outs, sems = refs[: len(operands)], refs[len(operands) : -1], refs[-1]
        started = [
            pltpu.make_async_copy(ins[i].at[at], outs[o].at[to], sems.at[n])
            for n, (i, at, o, to) in enumerate(moves(lax.axis_index("x"), lax.axis_index("y")))
        ]
        for copy in started:
            copy.start()
        for copy in started:
            copy.wait()

    dtype = operands[0].dtype
    total = sum(functools.reduce(lambda a, b: a * b, shape) for shape in out_shapes) * 2
    return pl.pallas_call(
        kernel,
        out_shape=[jax.ShapeDtypeStruct(shape, dtype) for shape in out_shapes],
        in_specs=[pl.BlockSpec(memory_space=pltpu.HBM)] * len(operands),
        out_specs=[pl.BlockSpec(memory_space=pltpu.VMEM)] * len(out_shapes),
        scratch_shapes=[pltpu.SemaphoreType.DMA((count,))],
        compiler_params=pltpu.CompilerParams(vmem_limit_bytes=2 * total + (4 << 20)),
        cost_estimate=pl.CostEstimate(flops=0, bytes_accessed=2 * total, transcendentals=0),
    )(*operands)


def near(block, axis):
    return turn(block, axis, -1), turn(block, axis, 1)


def halves(*pairs):
    count, (rows, cols) = 2 * len(pairs), pairs[0][0].shape
    half = rows // 2

    def kernel(*refs):
        ins, outs, held, sems = refs[:count], refs[count : 2 * count], refs[-2], refs[-1]
        loads = [
            pltpu.make_async_copy(ins[n ^ 1].at[pl.ds(n % 2 * half, half)], held.at[n], sems.at[0, n])
            for n in range(count)
        ]
        stores = [pltpu.make_async_copy(held.at[n], outs[n], sems.at[1, n]) for n in range(count)]
        for load in loads:
            load.start()
        for load, store in zip(loads, stores):
            load.wait()
            store.start()
        for store in stores:
            store.wait()

    dtype = pairs[0][0].dtype
    return pl.pallas_call(
        kernel,
        out_shape=[jax.ShapeDtypeStruct((half, cols), dtype)] * count,
        in_specs=[pl.BlockSpec(memory_space=pltpu.HBM)] * count,
        out_specs=[pl.BlockSpec(memory_space=pltpu.HBM)] * count,
        scratch_shapes=[
            pltpu.VMEM((count, half, cols), dtype),
            pltpu.SemaphoreType.DMA((2, count)),
        ],
        compiler_params=pltpu.CompilerParams(vmem_limit_bytes=12 << 20),
        cost_estimate=pl.CostEstimate(flops=0, bytes_accessed=4 * count * half * cols, transcendentals=0),
    )(*(block for pair in pairs for block in pair))


def opposite(upper, lower, axis):
    return turn(upper, axis, 1), turn(lower, axis, -1)


def first_ring(blocks, along_y):
    size, cols = blocks[0].shape

    def moves(x, y):
        place = y if along_y else x
        at = [lax.rem(place + step, RING) * size for step in range(RING)]
        spans = ((at[0], size), (at[1], size), (at[2], size // 2), (at[2] + size // 2, size // 2), (at[3], size))
        return [(i, pl.ds(0, length), 0, pl.ds(start, length)) for i, (start, length) in enumerate(spans)]

    return copies(moves, [(4 * size, cols)], *blocks)[0]


def second_moves(place, along_y, size):
    found = []
    for i, (step, parts) in enumerate(((0, range(4)), (1, range(4)), (2, (0, 1)), (2, (2, 3)), (3, range(4)))):
        outer = lax.rem(place + step, RING)
        for k, inner in enumerate(parts):
            at = inner * 4 + outer if along_y else outer * 4 + inner
            found.append((i, pl.ds(k * size, size), at * size))
    return found


def second_rings(a_blocks, b_blocks):
    size, cols = a_blocks[0].shape[0] // 4, a_blocks[0].shape[1]
    count = len(second_moves(0, True, size))

    def kernel(*refs):
        blocks, outs, sems = refs[:10], refs[10:12], refs[12]
        c = lax.axis_index("c")

        def move(n, out):
            moves = second_moves(lax.axis_index("y" if n == 0 else "x"), n == 0, size)
            return [
                pltpu.make_async_copy(blocks[5 * n + i].at[at], out.at[pl.ds(to, size)], sems.at[n, m])
                for m, (i, at, to) in enumerate(moves)
            ]

        for first in range(2):

            @pl.when(c == first)
            def _(first=first):
                started = move(first, outs[0]) + move(1 - first, outs[1])
                for copy in started:
                    copy.start()
                for copy in started:
                    copy.wait()

    return pl.pallas_call(
        kernel,
        out_shape=[jax.ShapeDtypeStruct((16 * size, cols), a_blocks[0].dtype)] * 2,
        in_specs=[pl.BlockSpec(memory_space=pltpu.HBM)] * 10,
        out_specs=[pl.BlockSpec(memory_space=pltpu.VMEM)] * 2,
        scratch_shapes=[pltpu.SemaphoreType.DMA((2, count))],
        compiler_params=pltpu.CompilerParams(vmem_limit_bytes=20 << 20),
        cost_estimate=pl.CostEstimate(flops=0, bytes_accessed=128 * size * cols, transcendentals=0),
    )(*a_blocks, *b_blocks)


def pick(rows, bit):
    half = rows.shape[0] // 2
    return (
        lax.dynamic_slice_in_dim(rows, bit * half, half),
        lax.dynamic_slice_in_dim(rows, (1 - bit) * half, half),
    )


def join(mine, other, bit):
    return jnp.where(bit == 0, jnp.concatenate([mine, other]), jnp.concatenate([other, mine]))


def swap_half(rows, exponent, axis, bit, mask):
    (mine, other), (kept, given) = pick(rows, bit), pick(exponent, bit)
    width = other.shape[1]
    wide = jnp.pad(other, ((0, 0), (0, 16)))
    inside = lax.broadcasted_iota(jnp.int32, wide.shape, 1) < width
    sent = jnp.where(inside, wide * jnp.exp2(13.0 - given), given).astype(jnp.float16)
    return mine, kept, sent, swap(sent, axis, mask)


def add_half(mine, kept, got):
    width = mine.shape[1]
    theirs = got[:, width : width + 1].astype(jnp.float32)
    sums = mine + got[:, :width].astype(jnp.float32) * jnp.exp2(theirs - 13.0)
    return sums, jnp.maximum(kept, theirs) + 1.0


def matmul(left, right):
    return jnp.dot(left, right, preferred_element_type=jnp.float32)


def cross_product(left, right):
    return lax.dot_general(
        left, right, (((0,), (0,)), ((), ())), preferred_element_type=jnp.float32
    )


def local(activations, gradients, input_basis, output_basis):
    x, y, h, l, c = (lax.axis_index(axis) for axis in AXES)
    rows, act_width = activations.shape
    grad_width = gradients.shape[1]
    total_rows = rows * 32
    grad_part, act_part = grad_width // 4, act_width // 4
    part = grad_part + act_part

    partner = swap(gradients, "h", 1)
    partner_acts = swap(activations, "h", 1)
    basis = lax.all_gather(input_basis, ("x", "y"), axis=0, tiled=True)
    a_next, a_prev = near(gradients, "x")
    a_up, a_down = opposite(*halves((a_next, a_prev)), "x")
    b_next, b_prev = near(partner, "y")

    def owned(array, width):
        cols = [lax.dynamic_slice_in_dim(array, (2 * j + h) * width, width, 1) for j in range(2)]
        return jnp.stack(cols)[None]

    acts = jnp.concatenate([activations, partner_acts])
    lines = after(owned(acts, act_part), a_next, a_prev)
    lines = join(lines, after(swap(lines, "l", 1), b_next, b_prev), l & 1)
    b_up, b_down = opposite(*halves((b_next, b_prev)), "y")
    a_up, a_down = after((a_up, a_down), lines)
    first_a = first_ring((gradients, a_next, a_up, a_down, a_prev), False)
    first_b = first_ring((partner, b_next, b_up, b_down, b_prev), True)
    first_a, first_b = lax.optimization_barrier((first_a, first_b))
    a_next, a_prev = near(first_a, "y")
    b_next, b_prev = near(first_b, "x")

    lines = join(lines, after(swap(lines, "l", 2), first_a, first_b), l >> 1)
    other = swap(lines, "c", 1)
    act_rows = jnp.where(c == 0, jnp.stack([lines, other], 1), jnp.stack([other, lines], 1))
    act_rows = act_rows.reshape(16, 2 * rows, act_part).swapaxes(0, 1).reshape(2 * rows, 16 * act_part)
    part_in = matmul(act_rows, basis)
    other_in = swap(part_in, "h", 1)

    lines = after(jnp.concatenate([owned(gradients, grad_part), owned(partner, grad_part)]), first_a, first_b)
    lines = lines[None]
    line_one = swap(lines, "l", 1)
    line_two = swap(lines, "l", 2)
    line_three = swap(line_two, "l", 1)

    a_next, a_prev, b_next, b_prev = after((a_next, a_prev, b_next, b_prev), part_in, line_one)
    far_halves = halves((a_next, a_prev), (b_next, b_prev))
    a_up, a_down = opposite(*far_halves[:2], "y")
    b_up, b_down = opposite(*far_halves[2:], "x")
    other_in = after(other_in, far_halves)
    projected_in = part_in + jnp.concatenate([other_in[rows:], other_in[:rows]])
    in_squares = (projected_in * projected_in).astype(jnp.bfloat16)
    shared = jnp.concatenate([in_squares, acts], axis=1)
    a_up, a_down, b_up, b_down = after((a_up, a_down, b_up, b_down), shared, line_three)
    shared = lax.all_gather(shared, ("x", "y"), axis=0).reshape(16, 2, rows, 2 * act_width)

    half = total_rows // 2
    grads, grads_rest = second_rings(
        (first_a, a_next, a_up, a_down, a_prev), (first_b, b_next, b_up, b_down, b_prev)
    )
    part_out = matmul(grads_rest, output_basis)
    kept = matmul(after(grads, part_out), output_basis)
    sums = kept + swap(part_out, "c", 1)
    exponent = jnp.max(jnp.abs(sums), axis=1, keepdims=True)
    exponent = jnp.ceil(jnp.log2(jnp.maximum(exponent, 1e-30)))
    *mine, sent, got = swap_half(sums, exponent, "l", l & 1, 1)

    started = soon(gradients, sent)
    line_one, line_two, line_three = after((line_one, line_two, line_three), started)
    lines = join(join(lines, line_one, l & 1), join(line_two, line_three, l & 1), l >> 1)
    mine_lines = jnp.where(c == 0, lines[:, 0], lines[:, 1])
    other = swap(jnp.where(c == 0, lines[:, 1], lines[:, 0]), "c", 1)
    sides = jnp.where(c == 0, jnp.stack([mine_lines, other], 1), jnp.stack([other, mine_lines], 1))
    sides = sides.reshape(16, rows, grad_part)
    act_sides = jnp.where(c == 0, act_rows[:rows], act_rows[rows:])
    act_sides = act_sides.reshape(rows, 16, act_part).swapaxes(0, 1)
    sides = jnp.concatenate([sides, act_sides], axis=2)
    sides = lax.all_to_all(sides, ("x", "y"), 0, 0, tiled=True).reshape(half, grad_part + act_part)

    *mine, sent, got = swap_half(*add_half(*mine, got), "l", l >> 1, 2)
    sums, _ = add_half(*mine, got)
    squares = (sums * sums).astype(jnp.bfloat16)
    line_one, line_two = swap(squares, "l", 1), swap(squares, "l", 2)
    sides, shared = after((sides, shared), soon(gradients, squares))
    sides_rest = swap(sides, "c", 1)
    shared = [lax.dynamic_index_in_dim(shared, i, 1, keepdims=False).reshape(half, -1) for i in (c, 1 - c)]
    output_covariance = cross_product(grads, sides[:, :grad_part])
    line_two = after(line_two, output_covariance, sides_rest)
    line_three = swap(line_two, "l", 1)
    shared, sides_rest = after((shared, sides_rest), line_two)
    output_covariance += cross_product(grads_rest, sides_rest[:, :grad_part])
    output_covariance /= total_rows
    input_covariance = sum(
        cross_product(block[:, act_width:], side[:, grad_part:])
        for block, side in zip(shared, (sides, sides_rest))
    ) / total_rows
    line_three = after(line_three, output_covariance, input_covariance)
    squares = join(join(squares, line_two, l >> 1), join(line_one, line_three, l >> 1), l & 1)
    squares_rest = swap(squares, "c", 1)
    corrections = sum(
        cross_product(block[:, :act_width], out) for block, out in zip(shared, (squares, squares_rest))
    )
    return input_covariance, output_covariance, corrections / total_rows


def solution(mesh):
    fine = Mesh(mesh.devices.reshape(SIZES), AXES)
    tok, blk = ("x", "y", "h"), ("l", "c")
    return jax.shard_map(
        local,
        mesh=fine,
        in_specs=(P(tok, blk), P(tok, blk), P(tok, blk), P(blk, tok)),
        out_specs=(P(blk, tok), P(blk, tok), P(blk, tok)),
        check_vma=False,
    )
```
